512 devices in a mesh: wide: 32 (over z, x_lo, core), narrow: 16 (over y, x_hi).
Axes of the slice: x: 4 (x_hi: 2, x_lo: 2; x = x_hi * 2 + x_lo), y: 8, z: 8, core: 2. Of those that a mesh axis runs over, the one named last changes fastest.
Arguments:
- left_blocks: bfloat16 [32, 16, 24, 4096], P('wide', 'narrow'), may hold values from -0.59765625 to 0.59765625
- right_blocks: bfloat16 [32, 16, 16, 4096], P('wide', 'narrow'), may hold values from -0.75 to 0.75
- earlier: float32 [32, 16, 16, 4096], P('wide', 'narrow'), may hold values from -6 to 6
- current: float32 [32, 16, 16, 4096], P('wide', 'narrow'), may hold values from -6 to 6
- stack_left: int32 [32, 16, 4, 128], P('wide', 'narrow'), may hold values from 0 to 23
- stack_right: int32 [32, 16, 4, 128], P('wide', 'narrow'), may hold values from 0 to 15
- stack_result: int32 [32, 16, 4, 128], P('wide', 'narrow'), may hold values from 0 to 15
- stack_count: int32 [32, 16, 4], P('wide', 'narrow'), may hold values from 21 to 128, as said below
- keep: int32 [32, 16, 16], P('wide', 'narrow'), may hold values 0 or 1
- send_list: int32 [32, 16, 32, 1], P('wide', 'narrow'), may hold values from 0 to 15
Outputs:
- received: bfloat16 [32, 16, 32, 4096], P('wide', 'narrow')
The draws below stay inside these ranges and needn't reach their ends.
Inputs may be any that keep to these rules, and one draw needn't show every extreme that they name: `stack_count`: every device has at least 21 live slots in each shift, and some device in every draw has all 128.
All inputs are finite; a program needn't handle non-finite values. No bound on the sum of `keep` on one device may be relied on, other than what follows from the above.
Results may differ from the reference program's by a relative error of at most 0.001.
Values may be sent and summed in bfloat16 or wider, within the bound.
A program may use at most 64 MiB of HBM per device.

```python
import jax
import jax.numpy as jnp
from jax import lax

B = 64
NL = 24
NR = 16
NC = 16
NS = 128
CAP = 1
SHIFTS = 4
N_WIDE = 32
N_NARROW = 16


def draw_stack_count(key, part):
    key = jax.random.fold_in(key, 7)
    parts = jax.random.randint(key, (N_WIDE, N_NARROW, SHIFTS), 0, 6)
    counts = NS // (1 + parts)
    first_key = jax.random.fold_in(key, 11)
    spot = jax.random.randint(first_key, (), 0, N_WIDE * N_NARROW * SHIFTS)
    flat_counts = counts.reshape(-1)
    flat_counts = flat_counts.at[spot].set(NS)
    return flat_counts.reshape(N_WIDE, N_NARROW, SHIFTS).astype(jnp.int32)


def with_ends(entries, rng, smallest, largest):
    place = [jax.random.randint(jax.random.fold_in(rng, axis), (), 0, length) for axis, length in enumerate(entries.shape)]
    longest = entries.shape.index(max(entries.shape))
    beside = place[:longest] + [(place[longest] + 1) % entries.shape[longest]] + place[longest + 1:]
    return entries.at[tuple(place)].set(smallest).at[tuple(beside)].set(largest)


def block_levels(rng, extent, shards, least, largest):
    def one(position, blocks):
        heights = jax.random.uniform(jax.random.fold_in(jax.random.fold_in(rng, 6), position), (blocks,), jnp.float32, least / len(shards), largest / len(shards))
        return jnp.repeat(jnp.exp(heights), extent[position] // blocks).reshape((-1,) + (1,) * (len(extent) - position - 1))

    factor_of = one(*shards[0])
    for cut in shards[1:]:
        factor_of = factor_of * one(*cut)
    return factor_of


def gaussian(rng, shape, width, reach, shards=(), held_as=jnp.bfloat16):
    values = jax.random.normal(rng, shape, jnp.float32) * width
    if len(shards) > 0:
        values = block_levels(rng, shape, shards, -0.22, 0.18) * values
    return jnp.clip(values, min=-reach, max=reach).astype(held_as)


def setup_inputs(seed: int = 0) -> dict:
    key_of = jax.random.split(jax.random.key(seed), 11)
    left_blocks = gaussian(key_of[0], (N_WIDE, N_NARROW, NL, B * B), 0.1, 0.59765625, ((0, 32), (1, 16)))
    right_blocks = gaussian(key_of[1], (N_WIDE, N_NARROW, NR, B * B), 0.125, 0.75, ((0, 32), (1, 16)))
    earlier = gaussian(key_of[2], (N_WIDE, N_NARROW, NC, B * B), 1.0, 6.0, ((0, 32), (1, 16)), jnp.float32)
    current = gaussian(key_of[3], (N_WIDE, N_NARROW, NC, B * B), 1.0, 6.0, ((0, 32), (1, 16)), jnp.float32)
    stack_left = with_ends(jax.random.randint(key_of[4], (N_WIDE, N_NARROW, SHIFTS, NS), 0, NL), jax.random.fold_in(key_of[4], 1), 0, NL - 1).astype(jnp.int32)
    stack_right = with_ends(jax.random.randint(key_of[5], (N_WIDE, N_NARROW, SHIFTS, NS), 0, NR), jax.random.fold_in(key_of[5], 1), 0, NR - 1).astype(jnp.int32)
    stack_result = with_ends(jax.random.randint(key_of[6], (N_WIDE, N_NARROW, SHIFTS, NS), 0, NC), jax.random.fold_in(key_of[6], 1), 0, NC - 1).astype(jnp.int32)
    stack_count = draw_stack_count(jax.random.fold_in(key_of[10], 71), 0)
    keep = with_ends((jax.random.randint(key_of[8], (N_WIDE, N_NARROW, NC), 0, 4) < 3).astype(jnp.int32), jax.random.fold_in(key_of[8], 1), 0, 1)
    send_list = with_ends(jax.random.randint(key_of[9], (N_WIDE, N_NARROW, N_WIDE, CAP), 0, NC), jax.random.fold_in(key_of[9], 1), 0, NC - 1).astype(jnp.int32)
    return {"left_blocks": left_blocks, "right_blocks": right_blocks, "earlier": earlier, "current": current, "stack_left": stack_left, "stack_right": stack_right, "stack_result": stack_result, "stack_count": stack_count, "keep": keep, "send_list": send_list}


def device_term(args):
    left, right, sl, sr, sc, count = args
    group = min(256, NS)
    left_mat = left.reshape(NL, B, B)
    right_mat = right.reshape(NR, B, B)

    def add_group(g, acc):
        start = g * group
        il = lax.dynamic_slice_in_dim(sl, start, group)
        ir = lax.dynamic_slice_in_dim(sr, start, group)
        ic = lax.dynamic_slice_in_dim(sc, start, group)
        first = left_mat[il].astype(jnp.float32)
        second = right_mat[ir].astype(jnp.float32)
        prod = jnp.einsum("gij,gjk->gik", first, second)
        slots = start + jnp.arange(group, dtype=jnp.int32)
        live = (slots < count).astype(jnp.float32)
        prod = prod * live[:, None, None]
        return acc + jax.ops.segment_sum(prod.reshape(group, B * B), ic, num_segments=NC)

    return lax.fori_loop(0, NS // group, add_group, jnp.zeros((NC, B * B), jnp.float32))


def reference(left_blocks, right_blocks, earlier, current, stack_left, stack_right, stack_result, stack_count, keep, send_list):
    count_all = N_WIDE * N_NARROW

    def flat(x):
        return x.reshape((count_all,) + x.shape[2:])

    total = earlier
    for shift in range(SHIFTS):
        left_now = jnp.roll(left_blocks, -shift, axis=0)
        right_now = jnp.roll(right_blocks, -shift, axis=1)
        terms = lax.map(device_term, (flat(left_now), flat(right_now), flat(stack_left[:, :, shift]), flat(stack_right[:, :, shift]), flat(stack_result[:, :, shift]), stack_count[:, :, shift].reshape(count_all)))
        total = total + terms.reshape(N_WIDE, N_NARROW, NC, B * B)
    updated = ((1.5 * current - 0.5 * total) * keep.astype(jnp.float32)[..., None]).astype(jnp.bfloat16)
    picked = jax.vmap(jax.vmap(lambda blocks, lists: blocks[lists]))(updated, send_list)
    moved = jnp.transpose(picked, (2, 1, 0, 3, 4))
    return moved.reshape(N_WIDE, N_NARROW, N_WIDE * CAP, B * B)
```

```python
import functools

import jax
import jax.numpy as jnp
from jax import lax
from jax.experimental import pallas as pl
from jax.experimental.pallas import tpu as pltpu
from jax.sharding import PartitionSpec as P

MESH = pl.DeviceIdType.MESH
EDGE = 64
LANES = 128


def kernel(
    n_wide,
    n_narrow,
    shifts,
    l_ref,
    r_ref,
    e_ref,
    c_ref,
    sl_ref,
    sr_ref,
    sc_ref,
    cnt_ref,
    keep_ref,
    send_ref,
    out_ref,
    lbuf,
    rbuf,
    ebuf,
    cbuf,
    rq,
    rd,
    wsel,
    ahi,
    alo,
    wt,
    tot,
    upd,
    rows,
    outgoing,
    lsend,
    lrecv,
    rsend,
    rrecv,
    esem,
    asend,
    arecv,
):
    w = lax.axis_index("wide")
    n = lax.axis_index("narrow")
    nl = l_ref.shape[0]
    nr = r_ref.shape[0]
    nc = e_ref.shape[0]
    tiles = l_ref.shape[1] // LANES
    bf16, f32 = jnp.bfloat16, jnp.float32

    own_l = pltpu.make_async_copy(l_ref, lbuf.at[0], lrecv.at[0])
    own_l.start()
    get_e = pltpu.make_async_copy(e_ref, ebuf, esem.at[0])
    get_e.start()
    get_c = pltpu.make_async_copy(c_ref, cbuf, esem.at[1])
    get_c.start()

    barrier = pltpu.get_barrier_semaphore()

    def greet(k, carry):
        pl.semaphore_signal(
            barrier, inc=1, device_id={"wide": lax.rem(w + k, n_wide)}, device_id_type=MESH
        )
        return carry

    lax.fori_loop(1, n_wide, greet, 0)
    for k in range(1, shifts):
        for other in (n + k, n + n_narrow - k):
            pl.semaphore_signal(
                barrier, inc=1, device_id={"narrow": lax.rem(other, n_narrow)}, device_id_type=MESH
            )
    pl.semaphore_wait(barrier, n_wide - 1 + 2 * (shifts - 1))

    l_copies = []
    for k in range(1, shifts):
        copy = pltpu.make_async_remote_copy(
            src_ref=l_ref,
            dst_ref=lbuf.at[k],
            send_sem=lsend.at[k],
            recv_sem=lrecv.at[k],
            device_id={"wide": lax.rem(w + n_wide - k, n_wide)},
            device_id_type=MESH,
        )
        copy.start()
        l_copies.append(copy)

    lane = lax.broadcasted_iota(jnp.int32, (EDGE // 2, LANES), 1)
    low = lane < EDGE
    for t in range(tiles):
        rq[pl.ds(t, nr, stride=tiles), :] = r_ref[:, t * LANES : (t + 1) * LANES].astype(f32)
    for p in range(nr // 2):
        even = rq[(2 * p) * tiles : (2 * p + 1) * tiles, :]
        odd = rq[(2 * p + 1) * tiles : (2 * p + 2) * tiles, :]
        rd[pl.ds(p * EDGE, EDGE // 2, stride=2), :] = jnp.where(low, even, pltpu.roll(odd, EDGE, 1))
        rd[pl.ds(p * EDGE + 1, EDGE // 2, stride=2), :] = jnp.where(
            low, pltpu.roll(even, EDGE, 1), odd
        )
    rbuf[0] = rd[...].astype(bf16)

    r_copies = []
    for k in range(1, shifts):
        copy = pltpu.make_async_remote_copy(
            src_ref=rbuf.at[0],
            dst_ref=rbuf.at[k],
            send_sem=rsend.at[k],
            recv_sem=rrecv.at[k],
            device_id={"narrow": lax.rem(n + n_narrow - k, n_narrow)},
            device_id_type=MESH,
        )
        copy.start()
        r_copies.append(copy)

    slots = sl_ref.shape[1]
    slot = lax.broadcasted_iota(jnp.int32, (1, slots), 1)
    for s in range(shifts):
        live = slot < cnt_ref[0, s]
        cell = jnp.where(live, sr_ref[s : s + 1, :] * nc + sc_ref[s : s + 1, :], -1)
        cells = lax.broadcasted_iota(jnp.int32, (nr * nc, slots), 0) == cell
        lefts = lax.broadcasted_iota(jnp.int32, (nl, slots), 0) == sl_ref[s : s + 1, :]
        wsel[s] = lax.dot_general(
            cells.astype(f32).astype(bf16),
            lefts.astype(f32).astype(bf16),
            (((1,), (1,)), ((), ())),
            preferred_element_type=f32,
        ).astype(bf16)

    tot[...] = jnp.zeros_like(tot)
    lane_w = lax.broadcasted_iota(jnp.int32, (EDGE, LANES), 1)
    low_w = lane_w < EDGE

    def one_shift(s, carry):
        @pl.when(s > 0)
        def _():
            pltpu.make_async_copy(rbuf.at[s], rbuf.at[s], rrecv.at[s]).wait()

        def weights(p, carry):
            pair = rbuf[s, pl.ds(pl.multiple_of(p * EDGE, EDGE), EDGE), :].astype(f32)
            turned = pltpu.roll(pair, EDGE, 1)
            base = pl.multiple_of(p * 4 * EDGE, 4 * EDGE)
            wt[pl.ds(base, EDGE), :] = jnp.where(low_w, pair, 0.0).astype(bf16)
            wt[pl.ds(base + EDGE, EDGE), :] = jnp.where(low_w, 0.0, turned).astype(bf16)
            wt[pl.ds(base + 2 * EDGE, EDGE), :] = jnp.where(low_w, turned, 0.0).astype(bf16)
            wt[pl.ds(base + 3 * EDGE, EDGE), :] = jnp.where(low_w, 0.0, pair).astype(bf16)
            return carry

        lax.fori_loop(0, nr // 2, weights, 0)
        pltpu.make_async_copy(lbuf.at[s], lbuf.at[s], lrecv.at[s]).wait()
        sel = wsel[s]

        def spread(q, carry):
            cols = pl.multiple_of(q * 2 * LANES, 2 * LANES)
            a = jnp.dot(sel, lbuf[s, :, pl.ds(cols, 2 * LANES)], preferred_element_type=f32)
            hi = a.astype(bf16)
            lo = (a - hi.astype(f32)).astype(bf16)
            for h in range(2):
                at = pl.ds(pl.multiple_of((2 * q + h) * nc, nc), nc)
                for r in range(nr):
                    src = (slice(r * nc, (r + 1) * nc), slice(h * LANES, (h + 1) * LANES))
                    ahi[at, r * LANES : (r + 1) * LANES] = hi[src]
                    alo[at, r * LANES : (r + 1) * LANES] = lo[src]
            return carry

        lax.fori_loop(0, tiles // 2, spread, 0)

        def multiply(m, carry):
            at = pl.ds(pl.multiple_of(m * 128, 128), 128)
            tot[at, :] += jnp.dot(
                ahi[at, :], wt[...], preferred_element_type=f32
            ) + jnp.dot(alo[at, :], wt[...], preferred_element_type=f32)
            return carry

        lax.fori_loop(0, tiles * nc // 128, multiply, 0)
        return carry

    lax.fori_loop(0, shifts, one_shift, 0)

    get_e.wait()
    get_c.wait()
    eye = lax.broadcasted_iota(jnp.int32, (nc, nc), 0) == lax.broadcasted_iota(jnp.int32, (nc, nc), 1)
    keep = jnp.sum(jnp.where(eye, keep_ref[...].astype(f32), 0.0), axis=1, keepdims=True)
    for t in range(tiles):
        cols = slice(t * LANES, (t + 1) * LANES)
        total = ebuf[:, cols] + tot[t * nc : (t + 1) * nc, :]
        upd[:, cols] = ((1.5 * cbuf[:, cols] - 0.5 * total) * keep).astype(bf16)
    eye_w = lax.broadcasted_iota(jnp.int32, (n_wide, n_wide), 0) == lax.broadcasted_iota(
        jnp.int32, (n_wide, n_wide), 1
    )
    sends = jnp.sum(jnp.where(eye_w, send_ref[...].astype(f32), 0.0), axis=1, keepdims=True)
    pick = (
        (lax.broadcasted_iota(jnp.int32, (n_wide, nc), 1) == sends.astype(jnp.int32))
        .astype(f32)
        .astype(bf16)
    )
    for t in range(0, tiles, 4):
        picked = jnp.dot(pick, upd[:, t * LANES : (t + 4) * LANES], preferred_element_type=f32)
        for h in range(4):
            rows[pl.ds(t + h, n_wide, stride=tiles), :] = picked[:, h * LANES : (h + 1) * LANES]
    for d in range(n_wide):
        outgoing[d] = rows[d * tiles : (d + 1) * tiles, :].astype(bf16)

    keep_own = pltpu.make_async_copy(outgoing.at[w], out_ref.at[w], arecv.at[w])
    keep_own.start()

    def block_copy(k):
        d = lax.rem(w + k, n_wide)
        return pltpu.make_async_remote_copy(
            src_ref=outgoing.at[d],
            dst_ref=out_ref.at[w],
            send_sem=asend.at[d],
            recv_sem=arecv.at[w],
            device_id={"wide": d},
            device_id_type=MESH,
        )

    def send_block(k, carry):
        block_copy(k).start()
        return carry

    lax.fori_loop(1, n_wide, send_block, 0)

    for copy in l_copies:
        copy.wait_send()
    for copy in r_copies:
        copy.wait_send()
    keep_own.wait()

    def settle(k, carry):
        block_copy(k).wait_send()
        src = lax.rem(w + k, n_wide)
        pltpu.make_async_copy(out_ref.at[src], out_ref.at[src], arecv.at[src]).wait()
        return carry

    lax.fori_loop(1, n_wide, settle, 0)


def per_device(n_wide, n_narrow, left, right, earlier, current, sl, sr, sc, count, keep, send):
    left, right, earlier, current = left[0, 0], right[0, 0], earlier[0, 0], current[0, 0]
    sl, sr, sc = sl[0, 0], sr[0, 0], sc[0, 0]
    shifts = sl.shape[0]
    nl, flat = left.shape
    nr = right.shape[0]
    nc = earlier.shape[0]
    tiles = flat // LANES
    count = count.reshape(1, shifts)
    keep = keep.reshape(1, nc)
    send = send.reshape(1, n_wide)
    bf16, f32 = jnp.bfloat16, jnp.float32
    vmem = pl.BlockSpec(memory_space=pltpu.VMEM)
    smem = pl.BlockSpec(memory_space=pltpu.SMEM)
    hbm = pl.BlockSpec(memory_space=pl.ANY)
    dma = pltpu.SemaphoreType.DMA
    out = pl.pallas_call(
        functools.partial(kernel, n_wide, n_narrow, shifts),
        out_shape=jax.ShapeDtypeStruct((n_wide, tiles, LANES), bf16),
        in_specs=[hbm, vmem, hbm, hbm, vmem, vmem, vmem, smem, vmem, vmem],
        out_specs=hbm,
        scratch_shapes=[
            pltpu.VMEM((shifts, nl, flat), bf16),
            pltpu.VMEM((shifts, nr // 2 * EDGE, LANES), bf16),
            pltpu.VMEM((nc, flat), f32),
            pltpu.VMEM((nc, flat), f32),
            pltpu.VMEM((nr * tiles, LANES), f32),
            pltpu.VMEM((nr // 2 * EDGE, LANES), f32),
            pltpu.VMEM((shifts, nr * nc, nl), bf16),
            pltpu.VMEM((tiles * nc, nr * LANES), bf16),
            pltpu.VMEM((tiles * nc, nr * LANES), bf16),
            pltpu.VMEM((nr * LANES, LANES), bf16),
            pltpu.VMEM((tiles * nc, LANES), f32),
            pltpu.VMEM((nc, flat), bf16),
            pltpu.VMEM((n_wide * tiles, LANES), f32),
            pltpu.VMEM((n_wide, tiles, LANES), bf16),
            dma((shifts,)),
            dma((shifts,)),
            dma((shifts,)),
            dma((shifts,)),
            dma((2,)),
            dma((n_wide,)),
            dma((n_wide,)),
        ],
        compiler_params=pltpu.CompilerParams(
            collective_id=0, has_side_effects=True, vmem_limit_bytes=40 * 1024 * 1024
        ),
        cost_estimate=pl.CostEstimate(
            flops=2 * shifts * 4096 * 256 * 256 * 3, bytes_accessed=4 << 20, transcendentals=0
        ),
    )(left, right, earlier, current, sl, sr, sc, count, keep, send)
    return out.reshape(1, 1, n_wide, flat)


def solution(mesh):
    spec4 = P("wide", "narrow", None, None)
    spec3 = P("wide", "narrow", None)
    return jax.shard_map(
        functools.partial(per_device, mesh.shape["wide"], mesh.shape["narrow"]),
        mesh=mesh,
        in_specs=(spec4,) * 7 + (spec3, spec3, spec4),
        out_specs=spec4,
        check_vma=False,
    )
```

```python
import functools

import jax
import jax.numpy as jnp
from jax import lax
from jax.experimental import pallas as pl
from jax.experimental.pallas import tpu as pltpu
from jax.sharding import PartitionSpec as P

MESH = pl.DeviceIdType.MESH
EDGE = 64
LANES = 128
VMEM_MIB = 60


def kernel(
    n_wide,
    n_narrow,
    shifts,
    l_ref,
    r_ref,
    e_ref,
    c_ref,
    sl_hbm,
    sr_hbm,
    sc_hbm,
    cnt_hbm,
    keep_hbm,
    send_hbm,
    out_ref,
    sl_ref,
    sr_ref,
    sc_ref,
    cnt_ref,
    keep_ref,
    send_ref,
    lbuf,
    rraw,
    rbuf,
    ebuf,
    cbuf,
    rq,
    rd,
    wsel,
    both,
    wt,
    tot,
    upd,
    rows,
    outgoing,
    lsend,
    lrecv,
    rsend,
    rrecv,
    esem,
    asend,
    arecv,
):
    w = lax.axis_index("wide")
    n = lax.axis_index("narrow")
    nl = l_ref.shape[0]
    nr = r_ref.shape[0]
    nc = e_ref.shape[0]
    tiles = l_ref.shape[1] // LANES
    half = tiles * nc
    bf16, f32 = jnp.bfloat16, jnp.float32

    barrier = pltpu.get_barrier_semaphore()
    for k in range(1, shifts):
        for other in (n + k, n + n_narrow - k):
            pl.semaphore_signal(
                barrier, inc=1, device_id={"narrow": lax.rem(other, n_narrow)}, device_id_type=MESH
            )

    def greet(k, carry):
        pl.semaphore_signal(
            barrier, inc=1, device_id={"wide": lax.rem(w + k, n_wide)}, device_id_type=MESH
        )
        return carry

    lax.fori_loop(1, n_wide, greet, 0)

    get_r = pltpu.make_async_copy(r_ref, rraw, esem.at[0])
    get_r.start()
    own_l = pltpu.make_async_copy(l_ref, lbuf.at[0], lrecv.at[0])
    own_l.start()
    gets = []
    for i, (src, dst) in enumerate(
        (
            (sl_hbm, sl_ref),
            (sr_hbm, sr_ref),
            (sc_hbm, sc_ref),
            (cnt_hbm, cnt_ref),
            (keep_hbm, keep_ref),
            (send_hbm, send_ref),
            (e_ref, ebuf),
            (c_ref, cbuf),
        )
    ):
        copy = pltpu.make_async_copy(src, dst, esem.at[i + 1])
        copy.start()
        gets.append(copy)

    pl.semaphore_wait(barrier, n_wide - 1 + 2 * (shifts - 1))

    l_copies = []
    for k in range(1, shifts):
        copy = pltpu.make_async_remote_copy(
            src_ref=l_ref,
            dst_ref=lbuf.at[k],
            send_sem=lsend.at[k],
            recv_sem=lrecv.at[k],
            device_id={"wide": lax.rem(w + n_wide - k, n_wide)},
            device_id_type=MESH,
        )
        copy.start()
        l_copies.append(copy)

    get_r.wait()
    lane = lax.broadcasted_iota(jnp.int32, (EDGE // 2, LANES), 1)
    low = lane < EDGE
    for t in range(tiles):
        rq[pl.ds(t, nr, stride=tiles), :] = rraw[:, t * LANES : (t + 1) * LANES].astype(f32)
    for p in range(nr // 2):
        even = rq[(2 * p) * tiles : (2 * p + 1) * tiles, :]
        odd = rq[(2 * p + 1) * tiles : (2 * p + 2) * tiles, :]
        rd[pl.ds(p * EDGE, EDGE // 2, stride=2), :] = jnp.where(low, even, pltpu.roll(odd, EDGE, 1))
        rd[pl.ds(p * EDGE + 1, EDGE // 2, stride=2), :] = jnp.where(
            low, pltpu.roll(even, EDGE, 1), odd
        )
    rbuf[0] = rd[...].astype(bf16)

    r_copies = []
    for k in range(1, shifts):
        copy = pltpu.make_async_remote_copy(
            src_ref=rbuf.at[0],
            dst_ref=rbuf.at[k],
            send_sem=rsend.at[k],
            recv_sem=rrecv.at[k],
            device_id={"narrow": lax.rem(n + n_narrow - k, n_narrow)},
            device_id_type=MESH,
        )
        copy.start()
        r_copies.append(copy)

    for copy in gets:
        copy.wait()
    slots = sl_ref.shape[1]
    slot = lax.broadcasted_iota(jnp.int32, (1, slots), 1)
    for s in range(shifts):
        live = slot < cnt_ref[:, s : s + 1]
        cell = jnp.where(live, sr_ref[s : s + 1, :] * nc + sc_ref[s : s + 1, :], -1)
        cells = lax.broadcasted_iota(jnp.int32, (nr * nc, slots), 0) == cell
        lefts = lax.broadcasted_iota(jnp.int32, (nl, slots), 0) == sl_ref[s : s + 1, :]
        wsel[s] = lax.dot_general(
            cells.astype(f32).astype(bf16),
            lefts.astype(f32).astype(bf16),
            (((1,), (1,)), ((), ())),
            preferred_element_type=f32,
        ).astype(bf16)

    tot[...] = jnp.zeros_like(tot)
    low_w = lax.broadcasted_iota(jnp.int32, (EDGE, LANES), 1) < EDGE

    def one_shift(s, carry):
        @pl.when(s > 0)
        def _():
            pltpu.make_async_copy(rbuf.at[s], rbuf.at[s], rrecv.at[s]).wait()

        for p in range(nr // 2):
            pair = rbuf[s, p * EDGE : (p + 1) * EDGE, :].astype(f32)
            turned = pltpu.roll(pair, EDGE, 1)
            base = p * 4 * EDGE
            wt[base : base + EDGE, :] = jnp.where(low_w, pair, 0.0).astype(bf16)
            wt[base + EDGE : base + 2 * EDGE, :] = jnp.where(low_w, 0.0, turned).astype(bf16)
            wt[base + 2 * EDGE : base + 3 * EDGE, :] = jnp.where(low_w, turned, 0.0).astype(bf16)
            wt[base + 3 * EDGE : base + 4 * EDGE, :] = jnp.where(low_w, 0.0, pair).astype(bf16)
        pltpu.make_async_copy(lbuf.at[s], lbuf.at[s], lrecv.at[s]).wait()
        sel = wsel[s]
        for q in range(tiles // 2):
            a = jnp.dot(
                sel, lbuf[s, :, q * 2 * LANES : (q + 1) * 2 * LANES], preferred_element_type=f32
            )
            hi = a.astype(bf16)
            lo = (a - hi.astype(f32)).astype(bf16)
            for h in range(2):
                at = (2 * q + h) * nc
                for r in range(nr):
                    src = (slice(r * nc, (r + 1) * nc), slice(h * LANES, (h + 1) * LANES))
                    both[at : at + nc, r * LANES : (r + 1) * LANES] = hi[src]
                    both[half + at : half + at + nc, r * LANES : (r + 1) * LANES] = lo[src]
        v = jnp.dot(both[...], wt[...], preferred_element_type=f32)
        tot[...] += v[:half] + v[half:]
        return carry

    lax.fori_loop(0, shifts, one_shift, 0)

    eye = lax.broadcasted_iota(jnp.int32, (nc, nc), 0) == lax.broadcasted_iota(jnp.int32, (nc, nc), 1)
    keep = jnp.sum(jnp.where(eye, keep_ref[...].astype(f32), 0.0), axis=1, keepdims=True)
    for t in range(tiles):
        cols = slice(t * LANES, (t + 1) * LANES)
        total = ebuf[:, cols] + tot[t * nc : (t + 1) * nc, :]
        upd[:, cols] = ((1.5 * cbuf[:, cols] - 0.5 * total) * keep).astype(bf16)
    eye_w = lax.broadcasted_iota(jnp.int32, (n_wide, n_wide), 0) == lax.broadcasted_iota(
        jnp.int32, (n_wide, n_wide), 1
    )
    sends = jnp.sum(jnp.where(eye_w, send_ref[...].astype(f32), 0.0), axis=1, keepdims=True)
    pick = (
        (lax.broadcasted_iota(jnp.int32, (n_wide, nc), 1) == sends.astype(jnp.int32))
        .astype(f32)
        .astype(bf16)
    )
    for t in range(0, tiles, 4):
        picked = jnp.dot(pick, upd[:, t * LANES : (t + 4) * LANES], preferred_element_type=f32)
        for h in range(4):
            rows[pl.ds(t + h, n_wide, stride=tiles), :] = picked[:, h * LANES : (h + 1) * LANES]

    def send_block(k, carry):
        d = lax.rem(w + k, n_wide)
        outgoing[d] = rows[pl.ds(pl.multiple_of(d * tiles, tiles), tiles), :].astype(bf16)
        pltpu.make_async_remote_copy(
            src_ref=outgoing.at[d],
            dst_ref=out_ref.at[w],
            send_sem=asend.at[0],
            recv_sem=arecv.at[0],
            device_id={"wide": d},
            device_id_type=MESH,
        ).start()
        return carry

    lax.fori_loop(1, n_wide, send_block, 0)
    outgoing[w] = rows[pl.ds(pl.multiple_of(w * tiles, tiles), tiles), :].astype(bf16)
    pltpu.make_async_copy(outgoing.at[w], out_ref.at[w], arecv.at[0]).start()

    for copy in l_copies:
        copy.wait_send()
    for copy in r_copies:
        copy.wait_send()
    others = outgoing.at[pl.ds(0, n_wide - 1)]
    pltpu.make_async_copy(others, others, asend.at[0]).wait()
    pltpu.make_async_copy(outgoing, outgoing, arecv.at[0]).wait()


def per_device(n_wide, n_narrow, left, right, earlier, current, sl, sr, sc, count, keep, send):
    left, right, earlier, current = left[0, 0], right[0, 0], earlier[0, 0], current[0, 0]
    sl, sr, sc = sl[0, 0], sr[0, 0], sc[0, 0]
    shifts, slots = sl.shape
    nl, flat = left.shape
    nr = right.shape[0]
    nc = earlier.shape[0]
    tiles = flat // LANES
    count = count.reshape(1, shifts)
    keep = keep.reshape(1, nc)
    send = send.reshape(1, n_wide)
    bf16, f32, i32 = jnp.bfloat16, jnp.float32, jnp.int32
    hbm = pl.BlockSpec(memory_space=pl.ANY)
    dma = pltpu.SemaphoreType.DMA
    out = pl.pallas_call(
        functools.partial(kernel, n_wide, n_narrow, shifts),
        out_shape=jax.ShapeDtypeStruct((n_wide, tiles, LANES), bf16),
        in_specs=[hbm] * 10,
        out_specs=hbm,
        scratch_shapes=[
            pltpu.VMEM((shifts, slots), i32),
            pltpu.VMEM((shifts, slots), i32),
            pltpu.VMEM((shifts, slots), i32),
            pltpu.VMEM((1, shifts), i32),
            pltpu.VMEM((1, nc), i32),
            pltpu.VMEM((1, n_wide), i32),
            pltpu.VMEM((shifts, nl, flat), bf16),
            pltpu.VMEM((nr, flat), bf16),
            pltpu.VMEM((shifts, nr // 2 * EDGE, LANES), bf16),
            pltpu.VMEM((nc, flat), f32),
            pltpu.VMEM((nc, flat), f32),
            pltpu.VMEM((nr * tiles, LANES), f32),
            pltpu.VMEM((nr // 2 * EDGE, LANES), f32),
            pltpu.VMEM((shifts, nr * nc, nl), bf16),
            pltpu.VMEM((2 * tiles * nc, nr * LANES), bf16),
            pltpu.VMEM((nr * LANES, LANES), bf16),
            pltpu.VMEM((tiles * nc, LANES), f32),
            pltpu.VMEM((nc, flat), bf16),
            pltpu.VMEM((n_wide * tiles, LANES), f32),
            pltpu.VMEM((n_wide, tiles, LANES), bf16),
            dma((shifts,)),
            dma((shifts,)),
            dma((shifts,)),
            dma((shifts,)),
            dma((9,)),
            dma((1,)),
            dma((1,)),
        ],
        compiler_params=pltpu.CompilerParams(
            collective_id=0, has_side_effects=True, vmem_limit_bytes=VMEM_MIB * 1024 * 1024
        ),
        cost_estimate=pl.CostEstimate(
            flops=2 * shifts * flat * 256 * 256 * 3, bytes_accessed=4 << 20, transcendentals=0
        ),
    )(left, right, earlier, current, sl, sr, sc, count, keep, send)
    return out.reshape(1, 1, n_wide, flat)


def solution(mesh):
    spec4 = P("wide", "narrow", None, None)
    spec3 = P("wide", "narrow", None)
    return jax.shard_map(
        functools.partial(per_device, mesh.shape["wide"], mesh.shape["narrow"]),
        mesh=mesh,
        in_specs=(spec4,) * 7 + (spec3, spec3, spec4),
        out_specs=spec4,
        check_vma=False,
    )
```

```python
import functools

import jax
import jax.numpy as jnp
from jax import lax
from jax.experimental import pallas as pl
from jax.experimental.pallas import tpu as pltpu
from jax.sharding import PartitionSpec as P

MESH = pl.DeviceIdType.MESH
EDGE = 64
LANES = 128
VMEM_MIB = 56
RELAY = 1


def kernel(
    n_wide,
    n_narrow,
    shifts,
    l_ref,
    r_ref,
    e_ref,
    c_ref,
    sl_hbm,
    sr_hbm,
    sc_hbm,
    cnt_hbm,
    keep_hbm,
    send_hbm,
    out_ref,
    sl_ref,
    sr_ref,
    sc_ref,
    cnt_ref,
    keep_ref,
    send_ref,
    lbuf,
    rraw,
    rbuf,
    ebuf,
    cbuf,
    rq,
    rd,
    wsel,
    both,
    wt,
    tot,
    upd,
    rows,
    outgoing,
    lsend,
    lrecv,
    rsend,
    rrecv,
    esem,
    asend,
    arecv,
):
    w = lax.axis_index("wide")
    n = lax.axis_index("narrow")
    nl = l_ref.shape[0]
    nr = r_ref.shape[0]
    nc = e_ref.shape[0]
    tiles = l_ref.shape[1] // LANES
    half = tiles * nc
    bf16, f32 = jnp.bfloat16, jnp.float32

    barrier = pltpu.get_barrier_semaphore()
    for k in range(1, shifts - 1):
        for other in (n + k, n + n_narrow - k):
            pl.semaphore_signal(
                barrier, inc=1, device_id={"narrow": lax.rem(other, n_narrow)}, device_id_type=MESH
            )

    def greet(k, carry):
        pl.semaphore_signal(
            barrier, inc=1, device_id={"wide": lax.rem(w + k, n_wide)}, device_id_type=MESH
        )
        return carry

    lax.fori_loop(1, n_wide, greet, 0)

    get_r = pltpu.make_async_copy(r_ref, rraw, esem.at[0])
    get_r.start()
    own_l = pltpu.make_async_copy(l_ref, lbuf.at[0], lrecv.at[0])
    own_l.start()
    gets = []
    for i, (src, dst) in enumerate(
        (
            (sl_hbm, sl_ref),
            (sr_hbm, sr_ref),
            (sc_hbm, sc_ref),
            (cnt_hbm, cnt_ref),
            (keep_hbm, keep_ref),
            (send_hbm, send_ref),
            (e_ref, ebuf),
            (c_ref, cbuf),
        )
    ):
        copy = pltpu.make_async_copy(src, dst, esem.at[i + 1])
        copy.start()
        gets.append(copy)

    pl.semaphore_wait(barrier, n_wide - 1 + 2 * (shifts - 2))

    odd = lax.rem(w, 2)

    def send_left(src, slot, to, sem):
        return pltpu.make_async_remote_copy(
            src_ref=src,
            dst_ref=lbuf.at[slot],
            send_sem=lsend.at[sem],
            recv_sem=lrecv.at[slot],
            device_id={"wide": lax.rem(to + n_wide, n_wide)},
            device_id_type=MESH,
        )

    left_two = send_left(l_ref, 2, w - 2, 0)
    left_two.start()
    left_near = send_left(l_ref, 3 - 2 * odd, w - 3 + 2 * odd, 1)
    left_near.start()
    left_on = send_left(lbuf.at[2], 1 + 2 * odd, w + 1 - 2 * odd, 2)

    get_r.wait()
    lane = lax.broadcasted_iota(jnp.int32, (EDGE // 2, LANES), 1)
    low = lane < EDGE
    for t in range(tiles):
        rq[pl.ds(t, nr, stride=tiles), :] = rraw[:, t * LANES : (t + 1) * LANES].astype(f32)
    for p in range(nr // 2):
        even = rq[(2 * p) * tiles : (2 * p + 1) * tiles, :]
        odd = rq[(2 * p + 1) * tiles : (2 * p + 2) * tiles, :]
        rd[pl.ds(p * EDGE, EDGE // 2, stride=2), :] = jnp.where(low, even, pltpu.roll(odd, EDGE, 1))
        rd[pl.ds(p * EDGE + 1, EDGE // 2, stride=2), :] = jnp.where(
            low, pltpu.roll(even, EDGE, 1), odd
        )
    rbuf[0] = rd[...].astype(bf16)

    def send_right(src, slot, back, sem):
        return pltpu.make_async_remote_copy(
            src_ref=rbuf.at[src],
            dst_ref=rbuf.at[slot],
            send_sem=rsend.at[sem],
            recv_sem=rrecv.at[slot],
            device_id={"narrow": lax.rem(n + n_narrow - back, n_narrow)},
            device_id_type=MESH,
        )

    right_one = send_right(0, 1, 1, 0)
    right_one.start()
    right_two = send_right(0, 2, 2, 1)
    right_two.start()
    right_on = send_right(1, 3, 2, 2)

    for copy in gets:
        copy.wait()
    slots = sl_ref.shape[1]
    slot = lax.broadcasted_iota(jnp.int32, (1, slots), 1)
    for s in range(shifts):
        live = slot < cnt_ref[:, s : s + 1]
        cell = jnp.where(live, sr_ref[s : s + 1, :] * nc + sc_ref[s : s + 1, :], -1)
        cells = lax.broadcasted_iota(jnp.int32, (nr * nc, slots), 0) == cell
        lefts = lax.broadcasted_iota(jnp.int32, (nl, slots), 0) == sl_ref[s : s + 1, :]
        wsel[s] = lax.dot_general(
            cells.astype(f32).astype(bf16),
            lefts.astype(f32).astype(bf16),
            (((1,), (1,)), ((), ())),
            preferred_element_type=f32,
        ).astype(bf16)

    tot[...] = jnp.zeros_like(tot)
    low_w = lax.broadcasted_iota(jnp.int32, (EDGE, LANES), 1) < EDGE

    def one_shift(i, carry):
        s = i // 2 + 2 * lax.rem(i, 2)

        @pl.when(i == 1)
        def _():
            pltpu.make_async_copy(rbuf.at[1], rbuf.at[1], rrecv.at[1]).wait()
            right_on.start()
            pltpu.make_async_copy(lbuf.at[2], lbuf.at[2], lrecv.at[2]).wait()
            left_on.start()
            pltpu.make_async_copy(rbuf.at[2], rbuf.at[2], rrecv.at[2]).wait()

        @pl.when(i == 3)
        def _():
            pltpu.make_async_copy(rbuf.at[3], rbuf.at[3], rrecv.at[3]).wait()

        for p in range(nr // 2):
            pair = rbuf[s, p * EDGE : (p + 1) * EDGE, :].astype(f32)
            turned = pltpu.roll(pair, EDGE, 1)
            base = p * 4 * EDGE
            wt[base : base + EDGE, :] = jnp.where(low_w, pair, 0.0).astype(bf16)
            wt[base + EDGE : base + 2 * EDGE, :] = jnp.where(low_w, 0.0, turned).astype(bf16)
            wt[base + 2 * EDGE : base + 3 * EDGE, :] = jnp.where(low_w, turned, 0.0).astype(bf16)
            wt[base + 3 * EDGE : base + 4 * EDGE, :] = jnp.where(low_w, 0.0, pair).astype(bf16)

        @pl.when(i != 1)
        def _():
            pltpu.make_async_copy(lbuf.at[s], lbuf.at[s], lrecv.at[s]).wait()

        sel = wsel[s]
        for q in range(tiles // 2):
            a = jnp.dot(
                sel, lbuf[s, :, q * 2 * LANES : (q + 1) * 2 * LANES], preferred_element_type=f32
            )
            hi = a.astype(bf16)
            lo = (a - hi.astype(f32)).astype(bf16)
            for h in range(2):
                at = (2 * q + h) * nc
                for r in range(nr):
                    src = (slice(r * nc, (r + 1) * nc), slice(h * LANES, (h + 1) * LANES))
                    both[at : at + nc, r * LANES : (r + 1) * LANES] = hi[src]
                    both[half + at : half + at + nc, r * LANES : (r + 1) * LANES] = lo[src]
        v = jnp.dot(both[...], wt[...], preferred_element_type=f32)
        tot[...] += v[:half] + v[half:]
        return carry

    lax.fori_loop(0, shifts, one_shift, 0)

    eye = lax.broadcasted_iota(jnp.int32, (nc, nc), 0) == lax.broadcasted_iota(jnp.int32, (nc, nc), 1)
    keep = jnp.sum(jnp.where(eye, keep_ref[...].astype(f32), 0.0), axis=1, keepdims=True)
    for t in range(tiles):
        cols = slice(t * LANES, (t + 1) * LANES)
        total = ebuf[:, cols] + tot[t * nc : (t + 1) * nc, :]
        upd[:, cols] = ((1.5 * cbuf[:, cols] - 0.5 * total) * keep).astype(bf16)
    eye_w = lax.broadcasted_iota(jnp.int32, (n_wide, n_wide), 0) == lax.broadcasted_iota(
        jnp.int32, (n_wide, n_wide), 1
    )
    sends = jnp.sum(jnp.where(eye_w, send_ref[...].astype(f32), 0.0), axis=1, keepdims=True)
    pick = (
        (lax.broadcasted_iota(jnp.int32, (n_wide, nc), 1) == sends.astype(jnp.int32))
        .astype(f32)
        .astype(bf16)
    )
    for t in range(0, tiles, 4):
        picked = jnp.dot(pick, upd[:, t * LANES : (t + 4) * LANES], preferred_element_type=f32)
        for h in range(4):
            rows[pl.ds(t + h, n_wide, stride=tiles), :] = picked[:, h * LANES : (h + 1) * LANES]

    def send_block(k, carry):
        d = lax.rem(w + k, n_wide)
        outgoing[d] = rows[pl.ds(pl.multiple_of(d * tiles, tiles), tiles), :].astype(bf16)
        pltpu.make_async_remote_copy(
            src_ref=outgoing.at[d],
            dst_ref=out_ref.at[w],
            send_sem=asend.at[0],
            recv_sem=arecv.at[0],
            device_id={"wide": d},
            device_id_type=MESH,
        ).start()
        return carry

    lax.fori_loop(1, n_wide, send_block, 0)
    outgoing[w] = rows[pl.ds(pl.multiple_of(w * tiles, tiles), tiles), :].astype(bf16)
    pltpu.make_async_copy(outgoing.at[w], out_ref.at[w], arecv.at[0]).start()

    for copy in (left_two, left_near, left_on, right_one, right_two, right_on):
        copy.wait_send()
    others = outgoing.at[pl.ds(0, n_wide - 1)]
    pltpu.make_async_copy(others, others, asend.at[0]).wait()
    pltpu.make_async_copy(outgoing, outgoing, arecv.at[0]).wait()


def per_device(n_wide, n_narrow, left, right, earlier, current, sl, sr, sc, count, keep, send):
    left, right, earlier, current = left[0, 0], right[0, 0], earlier[0, 0], current[0, 0]
    sl, sr, sc = sl[0, 0], sr[0, 0], sc[0, 0]
    shifts, slots = sl.shape
    nl, flat = left.shape
    nr = right.shape[0]
    nc = earlier.shape[0]
    tiles = flat // LANES
    count = count.reshape(1, shifts)
    keep = keep.reshape(1, nc)
    send = send.reshape(1, n_wide)
    bf16, f32, i32 = jnp.bfloat16, jnp.float32, jnp.int32
    hbm = pl.BlockSpec(memory_space=pl.ANY)
    vmem = pl.BlockSpec(memory_space=pltpu.VMEM)
    dma = pltpu.SemaphoreType.DMA
    operands = [
        pltpu.with_memory_space_constraint(x, pltpu.HBM)
        for x in (left, right, earlier, current, sl, sr, sc, count, keep, send)
    ]
    out = pl.pallas_call(
        functools.partial(kernel, n_wide, n_narrow, shifts),
        out_shape=pltpu.VMEM((n_wide, tiles, LANES), bf16),
        in_specs=[hbm] * 10,
        out_specs=vmem,
        scratch_shapes=[
            pltpu.VMEM((shifts, slots), i32),
            pltpu.VMEM((shifts, slots), i32),
            pltpu.VMEM((shifts, slots), i32),
            pltpu.VMEM((1, shifts), i32),
            pltpu.VMEM((1, nc), i32),
            pltpu.VMEM((1, n_wide), i32),
            pltpu.VMEM((shifts, nl, flat), bf16),
            pltpu.VMEM((nr, flat), bf16),
            pltpu.VMEM((shifts, nr // 2 * EDGE, LANES), bf16),
            pltpu.VMEM((nc, flat), f32),
            pltpu.VMEM((nc, flat), f32),
            pltpu.VMEM((nr * tiles, LANES), f32),
            pltpu.VMEM((nr // 2 * EDGE, LANES), f32),
            pltpu.VMEM((shifts, nr * nc, nl), bf16),
            pltpu.VMEM((2 * tiles * nc, nr * LANES), bf16),
            pltpu.VMEM((nr * LANES, LANES), bf16),
            pltpu.VMEM((tiles * nc, LANES), f32),
            pltpu.VMEM((nc, flat), bf16),
            pltpu.VMEM((n_wide * tiles, LANES), f32),
            pltpu.VMEM((n_wide, tiles, LANES), bf16),
            dma((shifts,)),
            dma((shifts,)),
            dma((shifts,)),
            dma((shifts,)),
            dma((9,)),
            dma((1,)),
            dma((1,)),
        ],
        compiler_params=pltpu.CompilerParams(
            collective_id=0, has_side_effects=True, vmem_limit_bytes=VMEM_MIB * 1024 * 1024
        ),
        cost_estimate=pl.CostEstimate(
            flops=2 * shifts * flat * 256 * 256 * 3, bytes_accessed=4 << 20, transcendentals=0
        ),
    )(*operands)
    return out.reshape(1, 1, n_wide, flat)


def solution(mesh):
    spec4 = P("wide", "narrow", None, None)
    spec3 = P("wide", "narrow", None)
    return jax.shard_map(
        functools.partial(per_device, mesh.shape["wide"], mesh.shape["narrow"]),
        mesh=mesh,
        in_specs=(spec4,) * 7 + (spec3, spec3, spec4),
        out_specs=spec4,
        check_vma=False,
    )
```

```python
import functools

import jax
import jax.numpy as jnp
from jax import lax
from jax.experimental import pallas as pl
from jax.experimental.pallas import tpu as pltpu
from jax.sharding import PartitionSpec as P

MESH = pl.DeviceIdType.MESH
EDGE = 64
LANES = 128
VMEM_MIB = 56
PARTS = 4


def kernel(
    n_wide,
    n_narrow,
    shifts,
    l_ref,
    r_ref,
    e_ref,
    c_ref,
    sl_hbm,
    sr_hbm,
    sc_hbm,
    cnt_hbm,
    keep_hbm,
    send_hbm,
    out_ref,
    sl_ref,
    sr_ref,
    sc_ref,
    cnt_ref,
    keep_ref,
    send_ref,
    lbuf,
    rraw,
    rbuf,
    ebuf,
    cbuf,
    rq,
    rd,
    wsel,
    both,
    wt,
    tot,
    upd,
    rows,
    outgoing,
    lsend,
    lrecv,
    rsend,
    rrecv,
    esem,
    asend,
    arecv,
):
    w = lax.axis_index("wide")
    n = lax.axis_index("narrow")
    nl = l_ref.shape[0]
    nr = r_ref.shape[0]
    nc = e_ref.shape[0]
    tiles = l_ref.shape[1] // LANES
    half = tiles * nc
    bf16, f32 = jnp.bfloat16, jnp.float32

    get_r = pltpu.make_async_copy(r_ref, rraw, esem.at[0])
    get_r.start()
    barrier = pltpu.get_barrier_semaphore()
    for k in range(1, shifts - 1):
        for other in (n + k, n + n_narrow - k):
            pl.semaphore_signal(
                barrier, inc=1, device_id={"narrow": lax.rem(other, n_narrow)}, device_id_type=MESH
            )

    def greet(k, carry):
        pl.semaphore_signal(
            barrier, inc=1, device_id={"wide": lax.rem(w + k, n_wide)}, device_id_type=MESH
        )
        return carry

    lax.fori_loop(1, n_wide, greet, 0)

    own_l = pltpu.make_async_copy(l_ref, lbuf.at[0], esem.at[9])
    own_l.start()
    gets = []
    for i, (src, dst) in enumerate(
        (
            (sl_hbm, sl_ref),
            (sr_hbm, sr_ref),
            (sc_hbm, sc_ref),
            (cnt_hbm, cnt_ref),
            (keep_hbm, keep_ref),
            (send_hbm, send_ref),
            (e_ref, ebuf),
            (c_ref, cbuf),
        )
    ):
        copy = pltpu.make_async_copy(src, dst, esem.at[i + 1])
        copy.start()
        gets.append(copy)

    get_r.wait()
    lane = lax.broadcasted_iota(jnp.int32, (EDGE // 2, LANES), 1)
    low = lane < EDGE
    for t in range(tiles):
        rq[pl.ds(t, nr, stride=tiles), :] = rraw[:, t * LANES : (t + 1) * LANES].astype(f32)
    for p in range(nr // 2):
        even = rq[(2 * p) * tiles : (2 * p + 1) * tiles, :]
        odd = rq[(2 * p + 1) * tiles : (2 * p + 2) * tiles, :]
        rd[pl.ds(p * EDGE, EDGE // 2, stride=2), :] = jnp.where(low, even, pltpu.roll(odd, EDGE, 1))
        rd[pl.ds(p * EDGE + 1, EDGE // 2, stride=2), :] = jnp.where(
            low, pltpu.roll(even, EDGE, 1), odd
        )
    rbuf[0] = rd[...].astype(bf16)

    odd = lax.rem(w, 2)

    def send_left(src, slot, to, sem):
        return pltpu.make_async_remote_copy(
            src_ref=src,
            dst_ref=lbuf.at[slot],
            send_sem=lsend.at[sem],
            recv_sem=lrecv.at[slot],
            device_id={"wide": lax.rem(to + n_wide, n_wide)},
            device_id_type=MESH,
        )

    def got_left(slot):
        return pltpu.make_async_copy(lbuf.at[slot], lbuf.at[slot], lrecv.at[slot])

    left_one = send_left(l_ref, 1, w - 1, 0)
    left_three = send_left(l_ref, 3, w - 3, 1)
    left_on = send_left(lbuf.at[3 - 2 * odd], 2, w + 1 - 2 * odd, 2)

    part = rbuf.shape[1] // PARTS

    def send_right(src, slot, back, sem, c):
        at = slice(c * part, (c + 1) * part)
        return pltpu.make_async_remote_copy(
            src_ref=rbuf.at[src, at],
            dst_ref=rbuf.at[slot, at],
            send_sem=rsend.at[sem, c],
            recv_sem=rrecv.at[slot, c],
            device_id={"narrow": lax.rem(n + n_narrow - back, n_narrow)},
            device_id_type=MESH,
        )

    def got_right(slot, c):
        ref = rbuf.at[slot, c * part : (c + 1) * part]
        return pltpu.make_async_copy(ref, ref, rrecv.at[slot, c])

    right_one = [send_right(0, 1, 1, 0, c) for c in range(PARTS)]
    right_two = [send_right(0, 2, 2, 1, c) for c in range(PARTS)]
    right_on = [send_right(1, 3, 2, 2, c) for c in range(PARTS)]

    pl.semaphore_wait(barrier, n_wide - 1 + 2 * (shifts - 2))
    for copy in right_one + [left_one]:
        copy.start()

    for copy in gets:
        copy.wait()
    slots = sl_ref.shape[1]
    slot = lax.broadcasted_iota(jnp.int32, (1, slots), 1)
    for s in range(shifts):
        live = slot < cnt_ref[:, s : s + 1]
        cell = jnp.where(live, sr_ref[s : s + 1, :] * nc + sc_ref[s : s + 1, :], -1)
        cells = lax.broadcasted_iota(jnp.int32, (nr * nc, slots), 0) == cell
        lefts = lax.broadcasted_iota(jnp.int32, (nl, slots), 0) == sl_ref[s : s + 1, :]
        wsel[s] = lax.dot_general(
            cells.astype(f32).astype(bf16),
            lefts.astype(f32).astype(bf16),
            (((1,), (1,)), ((), ())),
            preferred_element_type=f32,
        ).astype(bf16)

    tot[...] = jnp.zeros_like(tot)
    low_w = lax.broadcasted_iota(jnp.int32, (EDGE, LANES), 1) < EDGE

    def one_shift(i, carry):
        s = jnp.where(i < 2, i, 2 + lax.rem(i + odd, 2))

        @pl.when(i == 1)
        def _():
            for copy in right_one:
                copy.wait_send()
            for copy in [left_three] + right_two:
                copy.start()
            for c in range(PARTS):
                got_right(1, c).wait()
                right_on[c].start()
            got_left(1).wait()

            @pl.when(odd == 1)
            def _():
                left_on.start()

        @pl.when(i == 2)
        def _():
            got_left(3).wait()

            @pl.when(odd == 0)
            def _():
                left_on.start()
                got_left(2).wait()

        @pl.when((i == 3) & (odd == 1))
        def _():
            got_left(2).wait()

        sel = wsel[s]
        for q in range(tiles // 2):
            a = jnp.dot(
                sel, lbuf[s, :, q * 2 * LANES : (q + 1) * 2 * LANES], preferred_element_type=f32
            )
            hi = a.astype(bf16)
            lo = (a - hi.astype(f32)).astype(bf16)
            for h in range(2):
                at = (2 * q + h) * nc
                for r in range(nr):
                    src = (slice(r * nc, (r + 1) * nc), slice(h * LANES, (h + 1) * LANES))
                    both[at : at + nc, r * LANES : (r + 1) * LANES] = hi[src]
                    both[half + at : half + at + nc, r * LANES : (r + 1) * LANES] = lo[src]

        @pl.when(i > 1)
        def _():
            for c in range(PARTS):
                got_right(s, c).wait()

        for p in range(nr // 2):
            pair = rbuf[s, p * EDGE : (p + 1) * EDGE, :].astype(f32)
            turned = pltpu.roll(pair, EDGE, 1)
            base = p * 4 * EDGE
            wt[base : base + EDGE, :] = jnp.where(low_w, pair, 0.0).astype(bf16)
            wt[base + EDGE : base + 2 * EDGE, :] = jnp.where(low_w, 0.0, turned).astype(bf16)
            wt[base + 2 * EDGE : base + 3 * EDGE, :] = jnp.where(low_w, turned, 0.0).astype(bf16)
            wt[base + 3 * EDGE : base + 4 * EDGE, :] = jnp.where(low_w, 0.0, pair).astype(bf16)
        v = jnp.dot(both[...], wt[...], preferred_element_type=f32)
        tot[...] += v[:half] + v[half:]
        return carry

    own_l.wait()
    lax.fori_loop(0, shifts, one_shift, 0)

    eye = lax.broadcasted_iota(jnp.int32, (nc, nc), 0) == lax.broadcasted_iota(jnp.int32, (nc, nc), 1)
    keep = jnp.sum(jnp.where(eye, keep_ref[...].astype(f32), 0.0), axis=1, keepdims=True)
    for t in range(tiles):
        cols = slice(t * LANES, (t + 1) * LANES)
        total = ebuf[:, cols] + tot[t * nc : (t + 1) * nc, :]
        upd[:, cols] = ((1.5 * cbuf[:, cols] - 0.5 * total) * keep).astype(bf16)
    eye_w = lax.broadcasted_iota(jnp.int32, (n_wide, n_wide), 0) == lax.broadcasted_iota(
        jnp.int32, (n_wide, n_wide), 1
    )
    sends = jnp.sum(jnp.where(eye_w, send_ref[...].astype(f32), 0.0), axis=1, keepdims=True)
    pick = (
        (lax.broadcasted_iota(jnp.int32, (n_wide, nc), 1) == sends.astype(jnp.int32))
        .astype(f32)
        .astype(bf16)
    )
    for t in range(0, tiles, 4):
        picked = jnp.dot(pick, upd[:, t * LANES : (t + 4) * LANES], preferred_element_type=f32)
        for h in range(4):
            rows[pl.ds(t + h, n_wide, stride=tiles), :] = picked[:, h * LANES : (h + 1) * LANES]

    def send_block(k, carry):
        d = lax.rem(w + k, n_wide)
        outgoing[d] = rows[pl.ds(pl.multiple_of(d * tiles, tiles), tiles), :].astype(bf16)
        pltpu.make_async_remote_copy(
            src_ref=outgoing.at[d],
            dst_ref=out_ref.at[w],
            send_sem=asend.at[0],
            recv_sem=arecv.at[0],
            device_id={"wide": d},
            device_id_type=MESH,
        ).start()
        return carry

    lax.fori_loop(1, n_wide, send_block, 0)
    outgoing[w] = rows[pl.ds(pl.multiple_of(w * tiles, tiles), tiles), :].astype(bf16)
    pltpu.make_async_copy(outgoing.at[w], out_ref.at[w], arecv.at[0]).start()

    for copy in [left_one, left_three, left_on] + right_two + right_on:
        copy.wait_send()
    others = outgoing.at[pl.ds(0, n_wide - 1)]
    pltpu.make_async_copy(others, others, asend.at[0]).wait()
    pltpu.make_async_copy(outgoing, outgoing, arecv.at[0]).wait()


def per_device(n_wide, n_narrow, left, right, earlier, current, sl, sr, sc, count, keep, send):
    left, right, earlier, current = left[0, 0], right[0, 0], earlier[0, 0], current[0, 0]
    sl, sr, sc = sl[0, 0], sr[0, 0], sc[0, 0]
    shifts, slots = sl.shape
    nl, flat = left.shape
    nr = right.shape[0]
    nc = earlier.shape[0]
    tiles = flat // LANES
    count = count.reshape(1, shifts)
    keep = keep.reshape(1, nc)
    send = send.reshape(1, n_wide)
    bf16, f32, i32 = jnp.bfloat16, jnp.float32, jnp.int32
    hbm = pl.BlockSpec(memory_space=pl.ANY)
    vmem = pl.BlockSpec(memory_space=pltpu.VMEM)
    dma = pltpu.SemaphoreType.DMA
    operands = [
        pltpu.with_memory_space_constraint(x, pltpu.HBM)
        for x in (left, right, earlier, current, sl, sr, sc, count, keep, send)
    ]
    out = pl.pallas_call(
        functools.partial(kernel, n_wide, n_narrow, shifts),
        out_shape=pltpu.VMEM((n_wide, tiles, LANES), bf16),
        in_specs=[hbm] * 10,
        out_specs=vmem,
        scratch_shapes=[
            pltpu.VMEM((shifts, slots), i32),
            pltpu.VMEM((shifts, slots), i32),
            pltpu.VMEM((shifts, slots), i32),
            pltpu.VMEM((1, shifts), i32),
            pltpu.VMEM((1, nc), i32),
            pltpu.VMEM((1, n_wide), i32),
            pltpu.VMEM((shifts, nl, flat), bf16),
            pltpu.VMEM((nr, flat), bf16),
            pltpu.VMEM((shifts, nr // 2 * EDGE, LANES), bf16),
            pltpu.VMEM((nc, flat), f32),
            pltpu.VMEM((nc, flat), f32),
            pltpu.VMEM((nr * tiles, LANES), f32),
            pltpu.VMEM((nr // 2 * EDGE, LANES), f32),
            pltpu.VMEM((shifts, nr * nc, nl), bf16),
            pltpu.VMEM((2 * tiles * nc, nr * LANES), bf16),
            pltpu.VMEM((nr * LANES, LANES), bf16),
            pltpu.VMEM((tiles * nc, LANES), f32),
            pltpu.VMEM((nc, flat), bf16),
            pltpu.VMEM((n_wide * tiles, LANES), f32),
            pltpu.VMEM((n_wide, tiles, LANES), bf16),
            dma((3,)),
            dma((shifts,)),
            dma((3, PARTS)),
            dma((shifts, PARTS)),
            dma((10,)),
            dma((1,)),
            dma((1,)),
        ],
        compiler_params=pltpu.CompilerParams(
            collective_id=0, has_side_effects=True, vmem_limit_bytes=VMEM_MIB * 1024 * 1024
        ),
        cost_estimate=pl.CostEstimate(
            flops=2 * shifts * flat * 256 * 256 * 3, bytes_accessed=4 << 20, transcendentals=0
        ),
    )(*operands)
    return out.reshape(1, 1, n_wide, flat)


def solution(mesh):
    spec4 = P("wide", "narrow", None, None)
    spec3 = P("wide", "narrow", None)
    return jax.shard_map(
        functools.partial(per_device, mesh.shape["wide"], mesh.shape["narrow"]),
        mesh=mesh,
        in_specs=(spec4,) * 7 + (spec3, spec3, spec4),
        out_specs=spec4,
        check_vma=False,
    )
```

```python
import functools

import jax
import jax.numpy as jnp
from jax import lax
from jax.experimental import pallas as pl
from jax.experimental.pallas import tpu as pltpu
from jax.sharding import PartitionSpec as P

MESH = pl.DeviceIdType.MESH
EDGE = 64
LANES = 128
VMEM_MIB = 56
PARTS = 4
SPLIT = 2


def kernel(
    n_wide,
    n_narrow,
    shifts,
    l_ref,
    r_ref,
    e_ref,
    c_ref,
    sl_hbm,
    sr_hbm,
    sc_hbm,
    cnt_hbm,
    keep_hbm,
    send_hbm,
    out_ref,
    sl_ref,
    sr_ref,
    sc_ref,
    cnt_ref,
    keep_ref,
    send_ref,
    lbuf,
    rraw,
    rbuf,
    ebuf,
    cbuf,
    rq,
    rd,
    wsel,
    both,
    wt,
    tot,
    upd,
    rows,
    keeps,
    picks,
    outgoing,
    lsend,
    lrecv,
    rsend,
    rrecv,
    esem,
    asend,
    arecv,
    word,
):
    w = lax.axis_index("wide")
    n = lax.axis_index("narrow")
    nl = l_ref.shape[0]
    nr = r_ref.shape[0]
    nc = e_ref.shape[0]
    tiles = l_ref.shape[1] // LANES
    bf16, f32 = jnp.bfloat16, jnp.float32

    get_r = pltpu.make_async_copy(r_ref, rraw, esem.at[0])
    get_r.start()
    barrier = pltpu.get_barrier_semaphore()
    for k in range(1, shifts - 1):
        for other in (n + k, n + n_narrow - k):
            pl.semaphore_signal(
                barrier, inc=1, device_id={"narrow": lax.rem(other, n_narrow)}, device_id_type=MESH
            )

    for k in range(1, shifts):
        for other in (w + k, w + n_wide - k):
            pl.semaphore_signal(
                barrier, inc=1, device_id={"wide": lax.rem(other, n_wide)}, device_id_type=MESH
            )

    words = []
    reach = shifts - 1
    while 2 * reach + 1 < n_wide:
        words.append(reach)
        reach *= 2

    def say(i):
        for other in (w + words[i], w + n_wide - words[i]):
            pl.semaphore_signal(
                word.at[i], inc=1, device_id={"wide": lax.rem(other, n_wide)}, device_id_type=MESH
            )

    def hear(i):
        pl.semaphore_wait(word.at[i], 2)

    own_l = pltpu.make_async_copy(l_ref, lbuf.at[0], esem.at[9])
    own_l.start()
    gets = []
    for i, (src, dst) in enumerate(
        (
            (sl_hbm, sl_ref),
            (sr_hbm, sr_ref),
            (sc_hbm, sc_ref),
            (cnt_hbm, cnt_ref),
            (keep_hbm, keep_ref),
            (send_hbm, send_ref),
            (e_ref, ebuf),
            (c_ref, cbuf),
        )
    ):
        copy = pltpu.make_async_copy(src, dst, esem.at[i + 1])
        copy.start()
        gets.append(copy)

    odd = lax.rem(w, 2)

    def send_left(src, slot, to, sem):
        return pltpu.make_async_remote_copy(
            src_ref=src,
            dst_ref=lbuf.at[slot],
            send_sem=lsend.at[sem],
            recv_sem=lrecv.at[slot],
            device_id={"wide": lax.rem(to + n_wide, n_wide)},
            device_id_type=MESH,
        )

    def got_left(slot):
        return pltpu.make_async_copy(lbuf.at[slot], lbuf.at[slot], lrecv.at[slot])

    left_one = send_left(l_ref, 1, w - 1, 0)
    left_three = send_left(l_ref, 3, w - 3, 1)
    left_on = send_left(lbuf.at[3 - 2 * odd], 2, w + 1 - 2 * odd, 2)


    get_r.wait()
    lane = lax.broadcasted_iota(jnp.int32, (EDGE // 2, LANES), 1)
    low = lane < EDGE
    for t in range(tiles):
        rq[pl.ds(t, nr, stride=tiles), :] = rraw[:, t * LANES : (t + 1) * LANES].astype(f32)
    for p in range(nr // 2):
        first = rq[(2 * p) * tiles : (2 * p + 1) * tiles, :]
        second = rq[(2 * p + 1) * tiles : (2 * p + 2) * tiles, :]
        rd[pl.ds(p * EDGE, EDGE // 2, stride=2), :] = jnp.where(low, first, pltpu.roll(second, EDGE, 1))
        rd[pl.ds(p * EDGE + 1, EDGE // 2, stride=2), :] = jnp.where(
            low, pltpu.roll(first, EDGE, 1), second
        )
    rbuf[0] = rd[...].astype(bf16)

    part = rbuf.shape[1] // PARTS

    def send_right(src, slot, back, sem, c):
        at = slice(c * part, (c + 1) * part)
        return pltpu.make_async_remote_copy(
            src_ref=rbuf.at[src, at],
            dst_ref=rbuf.at[slot, at],
            send_sem=rsend.at[sem, c],
            recv_sem=rrecv.at[slot, c],
            device_id={"narrow": lax.rem(n + n_narrow - back, n_narrow)},
            device_id_type=MESH,
        )

    def got_right(slot, c):
        ref = rbuf.at[slot, c * part : (c + 1) * part]
        return pltpu.make_async_copy(ref, ref, rrecv.at[slot, c])

    right_one = [send_right(0, 1, 1, 0, c) for c in range(PARTS)]
    right_two = [send_right(0, 2, 2, 1, c) for c in range(PARTS)]
    right_on = [send_right(1, 3, 2, 2, c) for c in range(PARTS)]

    pl.semaphore_wait(barrier, 2 * (shifts - 1) + 2 * (shifts - 2))
    early = right_one + [left_one]
    late = [left_three] + right_two
    for copy in early:
        copy.start()
    say(0)

    for copy in gets:
        copy.wait()
    slots = sl_ref.shape[1]
    slot = lax.broadcasted_iota(jnp.int32, (1, slots), 1)
    for s in range(shifts):
        live = slot < cnt_ref[:, s : s + 1]
        cell = jnp.where(live, sr_ref[s : s + 1, :] * nc + sc_ref[s : s + 1, :], -1)
        cells = lax.broadcasted_iota(jnp.int32, (nr * nc, slots), 0) == cell
        lefts = lax.broadcasted_iota(jnp.int32, (nl, slots), 0) == sl_ref[s : s + 1, :]
        wsel[s] = lax.dot_general(
            cells.astype(f32).astype(bf16),
            lefts.astype(f32).astype(bf16),
            (((1,), (1,)), ((), ())),
            preferred_element_type=f32,
        ).astype(bf16)

    tot[...] = jnp.zeros_like(tot)
    low_w = lax.broadcasted_iota(jnp.int32, (EDGE, LANES), 1) < EDGE

    eye = lax.broadcasted_iota(jnp.int32, (nc, nc), 0) == lax.broadcasted_iota(jnp.int32, (nc, nc), 1)
    keep = jnp.sum(jnp.where(eye, keep_ref[...].astype(f32), 0.0), axis=1, keepdims=True)
    eye_w = lax.broadcasted_iota(jnp.int32, (n_wide, n_wide), 0) == lax.broadcasted_iota(
        jnp.int32, (n_wide, n_wide), 1
    )
    sends = jnp.sum(jnp.where(eye_w, send_ref[...].astype(f32), 0.0), axis=1, keepdims=True)
    pick = (
        (lax.broadcasted_iota(jnp.int32, (n_wide, nc), 1) == sends.astype(jnp.int32))
        .astype(f32)
        .astype(bf16)
    )
    keeps[...] = jnp.broadcast_to(keep, keeps.shape)
    picks[...] = pick

    group = tiles // SPLIT
    deep = group * nc

    def step(i, carry):
        early_step = i < 2 * SPLIT
        g = jnp.where(early_step, lax.rem(i, SPLIT), i // 2 - SPLIT)
        s = jnp.where(early_step, i // SPLIT, 2 + lax.rem(i + odd, 2))
        last = (i > 2 * SPLIT) & (lax.rem(i, 2) == 1)

        @pl.when(i == SPLIT)
        def _():
            hear(0)
            say(1)
            for copy in right_one:
                copy.wait_send()
            for copy in late:
                copy.start()
            for c in range(PARTS):
                got_right(1, c).wait()
                right_on[c].start()
            got_left(1).wait()

            @pl.when(odd == 1)
            def _():
                left_on.start()

            hear(1)
            say(2)

        @pl.when(i == 2 * SPLIT)
        def _():
            got_left(3).wait()

            @pl.when(odd == 0)
            def _():
                left_on.start()
                got_left(2).wait()

        @pl.when((i == 2 * SPLIT + 1) & (odd == 1))
        def _():
            got_left(2).wait()

        sel = wsel[s]
        for q in range(group // 2):
            cols = pl.ds(pl.multiple_of((g * group + 2 * q) * LANES, 2 * LANES), 2 * LANES)
            a = jnp.dot(sel, lbuf[s, :, cols], preferred_element_type=f32)
            hi = a.astype(bf16)
            lo = (a - hi.astype(f32)).astype(bf16)
            for h in range(2):
                at = (2 * q + h) * nc
                for r in range(nr):
                    src = (slice(r * nc, (r + 1) * nc), slice(h * LANES, (h + 1) * LANES))
                    both[at : at + nc, r * LANES : (r + 1) * LANES] = hi[src]
                    both[deep + at : deep + at + nc, r * LANES : (r + 1) * LANES] = lo[src]

        @pl.when((i >= 2 * SPLIT) & (i < 2 * SPLIT + 2))
        def _():
            for c in range(PARTS):
                got_right(s, c).wait()

        turn = lax.rem(s, 2)

        @pl.when(g == 0)
        def _():
            for p in range(nr // 2):
                pair = rbuf[s, p * EDGE : (p + 1) * EDGE, :].astype(f32)
                turned = pltpu.roll(pair, EDGE, 1)
                base = p * 4 * EDGE
                wt[turn, base : base + EDGE, :] = jnp.where(low_w, pair, 0.0).astype(bf16)
                wt[turn, base + EDGE : base + 2 * EDGE, :] = jnp.where(low_w, 0.0, turned).astype(bf16)
                wt[turn, base + 2 * EDGE : base + 3 * EDGE, :] = jnp.where(low_w, turned, 0.0).astype(bf16)
                wt[turn, base + 3 * EDGE : base + 4 * EDGE, :] = jnp.where(low_w, 0.0, pair).astype(bf16)

        v = jnp.dot(both[...], wt[turn], preferred_element_type=f32)
        part_rows = pl.ds(pl.multiple_of(g * deep, deep), deep)
        tot[part_rows, :] += v[:deep] + v[deep:]

        @pl.when(last)
        def _():
            @pl.when(g == 0)
            def _():
                hear(2)

            mine = pl.ds(pl.multiple_of(g * group, group), group)
            for t in range(group):
                cols = pl.ds(pl.multiple_of((g * group + t) * LANES, LANES), LANES)
                at = pl.ds(pl.multiple_of((g * group + t) * nc, nc), nc)
                total = ebuf[:, cols] + tot[at, :]
                upd[:, t * LANES : (t + 1) * LANES] = (
                    (1.5 * cbuf[:, cols] - 0.5 * total) * keeps[...]
                ).astype(bf16)
            for t in range(0, group, 4):
                picked = jnp.dot(
                    picks[...], upd[:, t * LANES : (t + 4) * LANES], preferred_element_type=f32
                )
                for h in range(4):
                    rows[pl.ds(t + h, n_wide, stride=group), :] = picked[
                        :, h * LANES : (h + 1) * LANES
                    ]

            def to_send(d):
                at = pl.ds(pl.multiple_of(d * group, group), group)
                outgoing[d, mine] = rows[at, :].astype(bf16)

            def send_block(j, carry):
                d = lax.rem(w + j + 1, n_wide)
                to_send(d)
                pltpu.make_async_remote_copy(
                    src_ref=outgoing.at[d, mine],
                    dst_ref=out_ref.at[w, mine],
                    send_sem=asend.at[0],
                    recv_sem=arecv.at[0],
                    device_id={"wide": d},
                    device_id_type=MESH,
                ).start()
                return carry

            lax.fori_loop(0, n_wide - 1, send_block, 0)
            to_send(w)
            pltpu.make_async_copy(outgoing.at[w, mine], out_ref.at[w, mine], arecv.at[0]).start()

        return carry

    own_l.wait()
    lax.fori_loop(0, shifts * SPLIT, step, 0)

    for copy in [left_one, left_three, left_on] + right_two + right_on:
        copy.wait_send()
    others = outgoing.at[pl.ds(0, n_wide - 1)]
    pltpu.make_async_copy(others, others, asend.at[0]).wait()
    pltpu.make_async_copy(outgoing, outgoing, arecv.at[0]).wait()


def per_device(n_wide, n_narrow, left, right, earlier, current, sl, sr, sc, count, keep, send):
    left, right, earlier, current = left[0, 0], right[0, 0], earlier[0, 0], current[0, 0]
    sl, sr, sc = sl[0, 0], sr[0, 0], sc[0, 0]
    shifts, slots = sl.shape
    nl, flat = left.shape
    nr = right.shape[0]
    nc = earlier.shape[0]
    tiles = flat // LANES
    count = count.reshape(1, shifts)
    keep = keep.reshape(1, nc)
    send = send.reshape(1, n_wide)
    bf16, f32, i32 = jnp.bfloat16, jnp.float32, jnp.int32
    hbm = pl.BlockSpec(memory_space=pl.ANY)
    vmem = pl.BlockSpec(memory_space=pltpu.VMEM)
    dma = pltpu.SemaphoreType.DMA
    operands = [
        pltpu.with_memory_space_constraint(x, pltpu.HBM)
        for x in (left, right, earlier, current, sl, sr, sc, count, keep, send)
    ]
    out = pl.pallas_call(
        functools.partial(kernel, n_wide, n_narrow, shifts),
        out_shape=pltpu.VMEM((n_wide, tiles, LANES), bf16),
        in_specs=[hbm] * 10,
        out_specs=vmem,
        scratch_shapes=[
            pltpu.VMEM((shifts, slots), i32),
            pltpu.VMEM((shifts, slots), i32),
            pltpu.VMEM((shifts, slots), i32),
            pltpu.VMEM((1, shifts), i32),
            pltpu.VMEM((1, nc), i32),
            pltpu.VMEM((1, n_wide), i32),
            pltpu.VMEM((shifts, nl, flat), bf16),
            pltpu.VMEM((nr, flat), bf16),
            pltpu.VMEM((shifts, nr // 2 * EDGE, LANES), bf16),
            pltpu.VMEM((nc, flat), f32),
            pltpu.VMEM((nc, flat), f32),
            pltpu.VMEM((nr * tiles, LANES), f32),
            pltpu.VMEM((nr // 2 * EDGE, LANES), f32),
            pltpu.VMEM((shifts, nr * nc, nl), bf16),
            pltpu.VMEM((2 * tiles // SPLIT * nc, nr * LANES), bf16),
            pltpu.VMEM((2, nr * LANES, LANES), bf16),
            pltpu.VMEM((tiles * nc, LANES), f32),
            pltpu.VMEM((nc, flat // SPLIT), bf16),
            pltpu.VMEM((n_wide * tiles // SPLIT, LANES), f32),
            pltpu.VMEM((nc, LANES), f32),
            pltpu.VMEM((n_wide, nc), bf16),
            pltpu.VMEM((n_wide, tiles, LANES), bf16),
            dma((3,)),
            dma((shifts,)),
            dma((3, PARTS)),
            dma((shifts, PARTS)),
            dma((10,)),
            dma((1,)),
            dma((1,)),
            pltpu.SemaphoreType.REGULAR((3,)),
        ],
        compiler_params=pltpu.CompilerParams(
            collective_id=0, has_side_effects=True, vmem_limit_bytes=VMEM_MIB * 1024 * 1024
        ),
        cost_estimate=pl.CostEstimate(
            flops=2 * shifts * flat * 256 * 256 * 3, bytes_accessed=4 << 20, transcendentals=0
        ),
    )(*operands)
    return out.reshape(1, 1, n_wide, flat)


def solution(mesh):
    spec4 = P("wide", "narrow", None, None)
    spec3 = P("wide", "narrow", None)
    return jax.shard_map(
        functools.partial(per_device, mesh.shape["wide"], mesh.shape["narrow"]),
        mesh=mesh,
        in_specs=(spec4,) * 7 + (spec3, spec3, spec4),
        out_specs=spec4,
        check_vma=False,
    )
```
